256 devices in a mesh: rep: 32 (over y_hi, z, core), fsdp: 8 (over x, y_lo).
Axes of the slice: x: 4, y: 4 (y_hi: 2, y_lo: 2; y = y_hi * 2 + y_lo), z: 8, core: 2. Of those that a mesh axis runs over, the one named last changes fastest.
Arguments:
- context: bfloat16 [65536, 2048], P(('rep', 'fsdp')), may hold values from -6 to 6
- cotangent: bfloat16 [65536, 4096], P(('rep', 'fsdp')), may hold values from -0.13183594 to 0.13183594
- out_weight: bfloat16 [2048, 4096], P('fsdp'), may hold values from -4 to 4
- error_buffer: bfloat16 [32, 2048, 4096], P('rep', 'fsdp'), may hold values from -1.5 to 1.5
- seed_basis: float32 [4096, 32], replicated, may hold values from -6 to 6
Outputs:
- ctx_grad: bfloat16 [65536, 2048], P(('rep', 'fsdp'))
- update: bfloat16 [2048, 4096], P('fsdp')
- new_error: bfloat16 [32, 2048, 4096], P('rep', 'fsdp')
- new_basis: float32 [4096, 32], replicated
The draws below stay inside these ranges and needn't reach their ends.
All inputs are finite; a program needn't handle non-finite values.
Results may differ from the reference program's by a relative error of at most 0.019.
Values may be sent and summed in bfloat16 or wider, within the bound.
No kernel may reach another device: no remote copies, remote signals or barrier semaphores. Data moves between devices by JAX's collectives and lax.ppermute only.
A program may use at most 128 MiB of HBM per device.

```python
import jax
import jax.numpy as jnp
from jax import lax

D = 4096
HD = 2048
RANK = 32
TOK_DEV = 256
TOKENS = 65536
N_REP = 32
N_FSDP = 8


def with_spikes(values, stream_key, source, target, blocks, factor):
    def block_of(axis_at):
        return (jnp.arange(values.shape[axis_at]) // (values.shape[axis_at] // blocks)).reshape((-1,) + (1,) * (values.ndim - 1 - axis_at))

    first = jax.random.permutation(stream_key, blocks)[block_of(target)]
    far = (block_of(target) + blocks // 2) % blocks
    return jnp.where((block_of(source) == first) | (block_of(source) == far), factor * values, values)


def block_levels(rng, dims, shards, smallest, top_value):
    gain = 1.0
    for position, parts in shards:
        draws = jax.random.uniform(jax.random.fold_in(jax.random.fold_in(rng, 6), position), (parts,), jnp.float32, smallest / len(shards), top_value / len(shards))
        gain = gain * jnp.repeat(jnp.exp(draws), dims[position] // parts).reshape((-1,) + (1,) * (len(dims) - 1 - position))
    return gain


def scatter_about(stream_key, dims, deviation, limit, pieces=(), held_as=jnp.bfloat16):
    gain = block_levels(stream_key, dims, pieces, -0.22, 0.18) if pieces else 1.0
    drawn = jax.random.normal(stream_key, dims, jnp.float32) * deviation * gain
    return jnp.minimum(jnp.maximum(drawn, -limit), limit).astype(held_as)


def noise_with(stream_key, extent, deviation, reach, shards, heavy, dtype=jnp.bfloat16):
    result = deviation * jax.random.normal(stream_key, extent, jnp.float32)
    if shards:
        result = result * block_levels(stream_key, extent, shards, -0.22, 0.18)
    return jnp.clip(with_spikes(result, jax.random.fold_in(stream_key, 3), *heavy), -reach, reach).astype(dtype)


def setup_inputs(seed: int = 0) -> dict:
    keys = jax.random.split(jax.random.key(seed), 6)
    context = scatter_about(keys[0], (TOKENS, HD), 1.0, 6.0, ((0, 256),))
    cotangent = scatter_about(keys[1], (TOKENS, D), ((TOK_DEV * N_FSDP) ** -0.5), 0.13183594, ((0, 256),))
    out_weight = scatter_about(keys[2], (HD, D), (max(1, D // (TOK_DEV * N_FSDP))) ** -0.5, 4.0, ((0, 8),))
    error_buffer = noise_with(keys[3], (N_REP, HD, D), 0.25, 1.5, ((0, 32), (1, 8)), (0, 2, 32, 2.75))
    seed_basis = scatter_about(keys[4], (D, RANK), 1.0, 6.0, (), jnp.float32)
    return dict(context=context, cotangent=cotangent, out_weight=out_weight, error_buffer=error_buffer, seed_basis=seed_basis)


def reference(context, cotangent, out_weight, error_buffer, seed_basis):
    highest = lax.Precision.HIGHEST
    ctx_grad = jnp.dot(cotangent.astype(jnp.float32), out_weight.T.astype(jnp.float32), preferred_element_type=jnp.float32).astype(jnp.bfloat16)
    ctx_blocks = context.reshape(N_REP, N_FSDP, TOK_DEV, HD)
    cot_blocks = cotangent.reshape(N_REP, N_FSDP, TOK_DEV, D)

    def replica(inputs):
        ctx_rep, cot_rep, err_rep = inputs

        def accumulate(running, block_pair):
            ctx_block, cot_block = block_pair
            partial_value = jnp.dot(ctx_block.T.astype(jnp.float32), cot_block.astype(jnp.float32), preferred_element_type=jnp.float32).astype(jnp.bfloat16)
            return (running + partial_value.astype(jnp.float32), None)
        summed, unused = lax.scan(accumulate, jnp.zeros((HD, D), jnp.float32), (ctx_rep, cot_rep))
        return summed + err_rep.astype(jnp.float32)
    merged = lax.map(replica, (ctx_blocks, cot_blocks, error_buffer))
    p_mean = jnp.sum(jnp.einsum('rhd,dk->rhk', merged, seed_basis, precision=highest), 0) / N_REP
    gram_matrix = jnp.dot(p_mean.T, p_mean, precision=highest)
    cholesky_factor = jnp.linalg.cholesky(gram_matrix)
    p_basis = lax.linalg.triangular_solve(cholesky_factor, p_mean, left_side=False, lower=True, transpose_a=True)
    new_basis = jnp.einsum('rhd,hk->dk', merged, p_basis, precision=highest) / N_REP
    low_rank = jnp.dot(p_basis, new_basis.T, precision=highest)
    update = low_rank.astype(jnp.bfloat16)
    new_error = (merged - low_rank[None]).astype(jnp.bfloat16)
    return (ctx_grad, update, new_error, new_basis)
```

```python
import jax
import jax.numpy as jnp
from jax import lax
from jax.sharding import Mesh
from jax.sharding import PartitionSpec as P

AXES = ("yh", "z", "c", "x", "yl")
FSDP = ("x", "yl")
F32 = jnp.float32
BF16 = jnp.bfloat16


def split3(a, axis):
    hi = a.astype(BF16)
    rest = a - hi.astype(F32)
    mid = rest.astype(BF16)
    low = (rest - mid.astype(F32)).astype(BF16)
    return jnp.concatenate([hi, mid, low], axis=axis)


def fold3(a):
    n = a.shape[0] // 3
    return a[:n] + (a[n : 2 * n] + a[2 * n :])


def dot(a, b, dims):
    return lax.dot_general(a, b, (dims, ((), ())), preferred_element_type=F32)


def all_sum(a):
    n = lax.axis_size(AXES)
    rows, cols = a.shape
    lanes = cols // 128
    per = n // lanes
    pieces = a.reshape(per, rows // per, lanes, 128).transpose(0, 2, 1, 3)
    pieces = pieces.reshape(n, rows // per, 128)
    mine = jnp.sum(lax.all_to_all(pieces, AXES, 0, 0, tiled=True), axis=0)
    full = lax.all_to_all(jnp.broadcast_to(mine[None], pieces.shape), AXES, 0, 0, tiled=True)
    full = full.reshape(per, lanes, rows // per, 128).transpose(0, 2, 1, 3)
    return full.reshape(rows, cols)


def body(context, cotangent, out_weight, error_buffer, seed_basis):
    highest = lax.Precision.HIGHEST
    n_x = lax.axis_size("x")
    n_rep = lax.axis_size(("yh", "z", "c"))
    x, yl = lax.axis_index("x"), lax.axis_index("yl")
    shard = x * 2 + yl
    tok, hd = context.shape
    dim = cotangent.shape[1]
    rows = hd // 8
    error = error_buffer[0]
    swap = [(0, 1), (1, 0)]

    weight_other = lax.ppermute(out_weight, "yl", swap)
    ctx_x = lax.all_to_all(context.reshape(tok, n_x, hd // n_x), "x", 1, 0, tiled=False)
    n_chunk = 2
    width = dim // n_chunk
    cot_g = [
        lax.all_gather(cotangent[:, i * width : (i + 1) * width], "x", axis=0, tiled=True)
        for i in range(n_chunk)
    ]

    seed3 = split3(seed_basis.T, 0)
    u = fold3(dot(seed3, cotangent, ((1,), (1,))))
    e_seed = fold3(dot(seed3, error, ((1,), (1,))))
    p_part = fold3(dot(split3(u, 0), context, ((1,), (0,))))
    at = (0, shard * rows)
    p_part = lax.dynamic_update_slice(
        p_part, lax.dynamic_slice(p_part, at, e_seed.shape) + e_seed, at
    )
    p_mean = all_sum(p_part) / n_rep
    p_rows = lax.dynamic_slice(p_mean, at, (p_mean.shape[0], rows))

    p3 = split3(p_mean, 0)
    v = fold3(dot(p3, context, ((1,), (1,))))
    q_part = fold3(
        dot(split3(v, 0), cotangent, ((1,), (0,))) + dot(split3(p_rows, 0), error, ((1,), (0,)))
    )
    q_sum = all_sum(q_part) / n_rep

    gram = lax.dot_general(p_mean, p_mean, (((1,), (1,)), ((), ())), precision=highest)
    chol = jnp.linalg.cholesky(gram)
    inv = lax.linalg.triangular_solve(
        chol, jnp.eye(gram.shape[0], dtype=F32), left_side=True, lower=True
    )
    p_basis = jnp.dot(inv, p_rows, precision=highest)
    new_basis = jnp.dot(inv, q_sum, precision=highest)

    ctx_x = ctx_x.reshape(n_x * tok, hd // n_x)
    ctx_mine = lax.dynamic_slice(ctx_x, (0, yl * rows), (n_x * tok, rows))
    ctx_other = lax.dynamic_slice(ctx_x, (0, (1 - yl) * rows), (n_x * tok, rows))
    merged = []
    own, oth = 0.0, 0.0
    for i, cg in enumerate(cot_g):
        sent = dot(ctx_other, cg, ((0,), (0,))).astype(BF16)
        got = lax.ppermute(sent, "yl", swap)
        kept = dot(ctx_mine, cg, ((0,), (0,)))
        cols = slice(i * width, (i + 1) * width)
        merged.append(kept + got.astype(F32) + error[:, cols].astype(F32))
        own = own + dot(cg, out_weight[:, cols], ((1,), (1,)))
        oth = oth + dot(cg, weight_other[:, cols], ((1,), (1,)))
    merged = jnp.concatenate(merged, axis=1)

    own, oth = own.astype(BF16), oth.astype(BF16)
    both = jnp.where(yl == 0, jnp.stack([own, oth], 1), jnp.stack([oth, own], 1))
    both = both.reshape(n_x, tok, 2 * rows)
    ctx_grad = lax.all_to_all(both, "x", 0, 0, tiled=True)
    ctx_grad = ctx_grad.transpose(1, 0, 2).reshape(tok, hd)

    low_rank = lax.dot_general(p_basis, new_basis, (((0,), (0,)), ((), ())), precision=highest)
    update = low_rank.astype(BF16)
    new_error = (merged - low_rank)[None].astype(BF16)
    return (ctx_grad, update, new_error, new_basis.T)


def solution(mesh):
    fine = Mesh(mesh.devices.reshape(2, 8, 2, 4, 2), AXES)
    rep = ("yh", "z", "c")
    return jax.shard_map(
        body,
        mesh=fine,
        in_specs=(P(AXES, None), P(AXES, None), P(FSDP, None), P(rep, FSDP, None), P()),
        out_specs=(P(AXES, None), P(FSDP, None), P(rep, FSDP, None), P()),
        check_vma=False,
    )
```

```python
import functools

import jax
import jax.numpy as jnp
from jax import lax
from jax.experimental import pallas as pl
from jax.experimental.pallas import tpu as pltpu
from jax.sharding import Mesh
from jax.sharding import PartitionSpec as P

AXES = ("yh", "z", "c", "x", "yl")
FSDP = ("x", "yl")
REP = ("yh", "z", "c")
F32 = jnp.float32
BF16 = jnp.bfloat16
SWAP = [(0, 1), (1, 0)]
TOK = 256
ROWS = 256
HD = 2048
DIM = 4096
RANK = 32
N_REP = 32
SPLIT = (2560, 1536)
STARTS = (0, 2560)
TILE = 512
FTILE = 512
VMEM = 60 << 20
NT = (((1,), (1,)), ((), ()))
NN = (((1,), (0,)), ((), ()))
TN = (((0,), (0,)), ((), ()))
RIGHT = [(0, 1), (1, 2), (2, 3), (3, 0)]
LEFT = [(1, 0), (2, 1), (3, 2), (0, 3)]
OPPOSITE = [(0, 2), (1, 3), (2, 0), (3, 1)]
fence = lax.optimization_barrier


def dot(a, b, dims):
    return lax.dot_general(a, b, dims, preferred_element_type=F32)


def terms(a):
    hi = a.astype(BF16)
    rest = a - hi.astype(F32)
    mid = rest.astype(BF16)
    return hi, mid, (rest - mid.astype(F32)).astype(BF16)


def split3(a):
    return jnp.concatenate(terms(a), axis=0)


def fold3(a):
    n = a.shape[0] // 3
    return a[:n] + (a[n : 2 * n] + a[2 * n :])


def left6(a):
    hi, mid, low = terms(a)
    return jnp.concatenate([hi, hi, mid, hi, mid, low], axis=0)


def right6(a):
    hi, mid, low = terms(a)
    return jnp.concatenate([hi, mid, hi, low, mid, hi], axis=0)


def params(size=VMEM):
    return pltpu.CompilerParams(vmem_limit_bytes=size)


def cost(flops, size):
    return pl.CostEstimate(flops=flops, bytes_accessed=size, transcendentals=0)


def to_tiles(src, row, out):
    lanes = src.shape[1] // 128
    for i in range(2):
        part = src[pl.ds(pl.multiple_of(row + 8 * i, 8), 8), :]
        for j in range(lanes):
            out[i * lanes + j] = part[:, j * 128 : (j + 1) * 128]


def from_tiles(t, row, dst):
    lanes = dst.shape[1] // 128
    for i in range(2):
        for j in range(lanes):
            dst[pl.ds(pl.multiple_of(row + 8 * i, 8), 8), j * 128 : (j + 1) * 128] = t[
                i * lanes + j
            ]


def copies(sems, pairs):
    started = []
    for i, (src, dst) in enumerate(pairs):
        copy = pltpu.make_async_copy(src, dst, sems.at[i])
        copy.start()
        started.append(copy)
    return started


def wait(started):
    for copy in started:
        copy.wait()


def call(kernel, name, ins, outs, scratch, flops, size, alias=None):
    spec = lambda inside: pl.BlockSpec(memory_space=pltpu.VMEM if inside else pl.ANY)
    return pl.pallas_call(
        kernel,
        in_specs=[pl.BlockSpec(memory_space=pltpu.SMEM)] + [spec(i) for _, i in ins[1:]],
        out_specs=[spec(i) for _, _, i in outs],
        out_shape=[jax.ShapeDtypeStruct(shape, dtype) for shape, dtype, _ in outs],
        scratch_shapes=scratch,
        input_output_aliases=alias or {},
        compiler_params=params(),
        cost_estimate=cost(flops, size),
        name=name,
    )(*[a for a, _ in ins])


DMA = lambda n: pltpu.SemaphoreType.DMA((n,))
PART = 1024
PARTS = DIM // PART


def left_kernel(at, seed, cot, err, ctx, keep, send, seed_v, cot_v, err_v, ctx_v, p, sems):
    sides = [slice(j * PART, (j + 1) * PART) for j in range(PARTS)]
    started = copies(
        sems,
        [(a.at[:, s], b.at[:, s]) for s in sides for a, b in ((seed, seed_v), (cot, cot_v), (err, err_v))]
        + [(ctx, ctx_v)],
    )
    u = e = 0.0
    for j, s in enumerate(sides):
        wait(started[3 * j : 3 * j + 3])
        s3 = split3(seed_v[:, s])
        u += dot(s3, cot_v[:, s], NT)
        e += dot(s3, err_v[:, s], NT)
    wait(started[-1:])
    p[...] = fold3(dot(split3(fold3(u)), ctx_v[...], NN))
    cols = pl.ds(pl.multiple_of((at[0] * 2 + at[1]) * ROWS, ROWS), ROWS)
    p[:, cols] += fold3(e)
    to_tiles(p, at[2] * 16, keep)
    to_tiles(p, (1 - at[2]) * 16, send)


def left_part(at, seed_t, cot, err, ctx):
    out = ((HD // 64, 8, 128), F32, True)
    return call(
        left_kernel,
        "left_part",
        [(at, True), (seed_t, False), (cot, False), (err, False), (ctx, False)],
        [out, out],
        [
            pltpu.VMEM((RANK, DIM), F32),
            pltpu.VMEM((TOK, DIM), BF16),
            pltpu.VMEM((ROWS, DIM), BF16),
            pltpu.VMEM((TOK, HD), BF16),
            pltpu.VMEM((RANK, HD), F32),
            DMA(3 * PARTS + 1),
        ],
        2 * 256 * 256 * 4096 * 3,
        6 << 20,
    )


def right_kernel(
    at, own, other, ctx, cot, err, keep, send, gram, rows, ctx_v, cot_v, err_v, p, q, sems
):
    sides = [slice(j * PART, (j + 1) * PART) for j in range(PARTS)]
    started = copies(
        sems,
        [(ctx, ctx_v)]
        + [(a.at[:, s], b.at[:, s]) for s in sides for a, b in ((cot, cot_v), (err, err_v))],
    )
    from_tiles(own, at[2] * 16, p)
    from_tiles(other, (1 - at[2]) * 16, p)
    p[...] = p[...] * (1.0 / N_REP)
    p3 = split3(p[...])
    mine = p[:, pl.ds(pl.multiple_of((at[0] * 2 + at[1]) * ROWS, ROWS), ROWS)]
    rows[...] = mine
    r3 = split3(mine)
    full = dot(p3, p3, NT)
    full = full[:RANK] + (full[RANK : 2 * RANK] + full[2 * RANK :])
    gram[...] = full[:, :RANK] + (full[:, RANK : 2 * RANK] + full[:, 2 * RANK :])
    wait(started[:1])
    v3 = split3(fold3(dot(p3, ctx_v[...], NT)))
    for j, s in enumerate(sides):
        wait(started[1 + 2 * j : 3 + 2 * j])
        q[:, s] = fold3(dot(v3, cot_v[:, s], NN) + dot(r3, err_v[:, s], NN))
    to_tiles(q, at[2] * 16, keep)
    to_tiles(q, (1 - at[2]) * 16, send)


def right_part(at, own, other, ctx, cot, err):
    out = ((DIM // 64, 8, 128), F32, True)
    return call(
        right_kernel,
        "right_part",
        [(at, True), (own, True), (other, True), (ctx, False), (cot, False), (err, False)],
        [out, out, ((RANK, RANK), F32, True), ((RANK, ROWS), F32, True)],
        [
            pltpu.VMEM((TOK, HD), BF16),
            pltpu.VMEM((TOK, DIM), BF16),
            pltpu.VMEM((ROWS, DIM), BF16),
            pltpu.VMEM((RANK, HD), F32),
            pltpu.VMEM((RANK, DIM), F32),
            DMA(2 * PARTS + 1),
        ],
        2 * 256 * 256 * 4096 * 3,
        6 << 20,
    )


def quarters_kernel(at, ctx, *rest):
    outs, ctx_v, sems = rest[:4], rest[4], rest[5]
    wait(copies(sems, [(ctx, ctx_v)]))
    for out, k in zip(outs, (0, 1, 3, 2)):
        lane = pl.multiple_of(lax.rem(at[0] + k, 4) * 2 * ROWS, 2 * ROWS)
        out[...] = ctx_v[:, pl.ds(lane, 2 * ROWS)].T


def quarters(at, ctx):
    return call(
        quarters_kernel,
        "quarters",
        [(at, True), (ctx, False)],
        [((2 * ROWS, TOK), BF16, True)] * 4,
        [pltpu.VMEM((TOK, HD), BF16), DMA(1)],
        0,
        2 << 20,
    )


def pick_kernel(at, src, dst, sems):
    n, cols = dst.shape
    rows = pl.ds(pl.multiple_of(at[2] * n, n), n)
    width = cols // 4
    sides = [pl.ds(i * width, width) for i in range(4)]
    wait(copies(sems, [(src.at[rows, s], dst.at[:, s]) for s in sides]))


def pick_half(at, a):
    rows, cols = a.shape
    outs = [((rows // 2, cols), a.dtype, True)]
    return call(pick_kernel, "pick_half", [(at, True), (a, False)], outs, [DMA(4)], 0, 2 << 20)[0]


def place_kernel(at, *refs):
    parts, dst, sems = refs[:4], refs[4], refs[5]
    width = parts[0].shape[1]
    pairs = []
    for part, k in zip(parts, (0, 3, 1, 2)):
        lane = pl.multiple_of(lax.rem(at[0] + k, 4) * width, width)
        pairs.append((part, dst.at[:, pl.ds(lane, width)]))
    wait(copies(sems, pairs))


def place(at, parts):
    tok, width = parts[0].shape
    ins = [(at, True)] + [(a, False) for a in parts]
    outs = [((tok, 4 * width), BF16, True)]
    return call(place_kernel, "place", ins, outs, [DMA(4)], 0, 2 << 20)[0]


def block_pairs(at, start, j, cot, others, buf, tile=None):
    here = pl.ds(j * TILE, TILE)
    tile = j if tile is None else tile
    pairs = [(cot.at[:, pl.ds(start + j * TILE, TILE)], buf.at[tile, pl.ds(0, TOK)])]
    for i, k in enumerate((3, 1, 2)):
        src = others[0].at[lax.rem(at[0] + k, 4), :, here] if len(others) == 1 else others[i].at[:, here]
        pairs.append((src, buf.at[tile, pl.ds((i + 1) * TOK, TOK)]))
    return pairs


def grad_kernel(start, count, n, at, *refs):
    ctx, cot, err, others = refs[:4], refs[4], refs[5], refs[6 : 6 + n]
    kept, sent, lhs, buf, err_v, out_k, out_s, in_sems, out_sems = refs[-9:]
    yl = at[1]
    pairs = []
    for k, block in enumerate(ctx):
        for i, row in enumerate((yl, 1 - yl)):
            rows = pl.ds(pl.multiple_of(row * ROWS, ROWS), ROWS)
            to = lhs.at[pl.ds(i * ROWS, ROWS), pl.ds(k * TOK, TOK)]
            pairs.append((block.at[rows, :], to))
    for j in range(count):
        pairs += block_pairs(at, start, j, cot, others, buf)
        pairs.append((err.at[:, pl.ds(start + j * TILE, TILE)], err_v.at[j]))
    started = copies(in_sems, pairs)
    wait(started[:8])
    done = []
    for j in range(count):
        wait(started[8 + 5 * j : 13 + 5 * j])
        out = dot(lhs[...], buf[j], NN)
        out_k[j] = (out[:ROWS] + err_v[j].astype(F32)).astype(BF16)
        out_s[j] = out[ROWS:].astype(BF16)
        done += copies(
            out_sems.at[pl.ds(2 * j, 2)],
            [
                (out_k.at[j], kept.at[:, pl.ds(j * TILE, TILE)]),
                (out_s.at[j], sent.at[:, pl.ds(j * TILE, TILE)]),
            ],
        )
    wait(done)


def grad_chunk(at, ctx, cot, err, others, start):
    width = others[0].shape[-1]
    count = width // TILE
    return call(
        functools.partial(grad_kernel, start, count, len(others)),
        "grad_chunk",
        [(at, True)] + [(a, False) for a in (*ctx, cot, err, *others)],
        [((ROWS, width), BF16, False), ((ROWS, width), BF16, False)],
        [
            pltpu.VMEM((2 * ROWS, 4 * TOK), BF16),
            pltpu.VMEM((count, 4 * TOK, TILE), BF16),
            pltpu.VMEM((count, ROWS, TILE), BF16),
            pltpu.VMEM((count, ROWS, TILE), BF16),
            pltpu.VMEM((count, ROWS, TILE), BF16),
            DMA(8 + 5 * count),
            DMA(2 * count),
        ],
        2 * 512 * 1024 * width,
        4 * 1024 * width,
    )


def ctx_kernel(sizes, at, cot, w_own, w_half, w_other, *refs):
    outs, (buf, wbuf, acc, sems) = refs[-8:-4], refs[-4:]
    pairs = []
    tile = 0
    for n, start, width in sizes:
        others, refs = refs[:n], refs[n:]
        for j in range(width // TILE):
            pairs += block_pairs(at, start, j, cot, others, buf, tile)
            cols = pl.ds(start + j * TILE, TILE)
            half = ROWS // 2
            for w, row, m in ((w_own, 0, ROWS), (w_half, ROWS, half), (w_other, ROWS + half, half)):
                pairs.append((w.at[:, cols], wbuf.at[tile, pl.ds(row, m)]))
            tile += 1
    started = copies(sems, pairs)
    for j in range(tile):
        wait(started[7 * j : 7 * j + 7])
        part = dot(buf[j], wbuf[j], NT)
        if j == 0:
            acc[...] = part
        else:
            acc[...] += part
    yl, c = at[1], at[2]
    half = ROWS // 2
    mine = pl.ds(pl.multiple_of(yl * ROWS, ROWS), ROWS)
    for k, out in enumerate(outs):
        tok = slice(k * TOK, (k + 1) * TOK)
        out[:, mine] = acc[tok, :ROWS].astype(BF16)
        for i, h in enumerate((c, 1 - c)):
            lane = pl.multiple_of((1 - yl) * ROWS + h * half, half)
            out[:, pl.ds(lane, half)] = acc[tok, ROWS + i * half : ROWS + (i + 1) * half].astype(
                BF16
            )


def ctx_blocks(at, cot, groups, weights):
    sizes = [(len(others), start, others[0].shape[-1]) for start, others in groups]
    count = DIM // TILE
    flat = [a for _, others in groups for a in others]
    return call(
        functools.partial(ctx_kernel, sizes),
        "ctx_blocks",
        [(at, True)] + [(a, False) for a in (cot, *weights, *flat)],
        [((TOK, 2 * ROWS), BF16, True)] * 4,
        [
            pltpu.VMEM((count, 4 * TOK, TILE), BF16),
            pltpu.VMEM((count, 2 * ROWS, TILE), BF16),
            pltpu.VMEM((4 * TOK, 2 * ROWS), F32),
            DMA(7 * count),
        ],
        2 * 512 * 1024 * DIM,
        4 * 1024 * DIM,
    )


def final_kernel(at, inv, rows, own, other, *refs):
    n = len(SPLIT)
    kept, got = refs[:n], refs[n : 2 * n]
    basis, update, new_err, q, kept_v, got_v, up_v, new_v, in_sems, out_sems = refs[2 * n :]
    sides = [slice(j * FTILE, (j + 1) * FTILE) for j in range(DIM // FTILE)]
    pairs = []
    for j, s in enumerate(sides):
        i = max(i for i in range(n) if STARTS[i] <= s.start)
        src = pl.ds(s.start - STARTS[i], FTILE)
        pairs += [(kept[i].at[:, src], kept_v.at[j]), (got[i].at[:, src], got_v.at[j])]
    started = copies(in_sems, pairs)
    from_tiles(own, at[2] * 16, q)
    from_tiles(other, (1 - at[2]) * 16, q)
    inv6 = left6(inv[...].T)
    pb = left6(dot(inv6, right6(rows[...]), TN))
    done = []
    for j, s in enumerate(sides):
        nb = dot(inv6, right6(q[:, s]), TN) * (1.0 / N_REP)
        basis[:, s] = nb
        low = dot(pb, right6(nb), TN)
        up_v[j] = low.astype(BF16)
        wait(started[2 * j : 2 * j + 2])
        new_v[j] = (kept_v[j].astype(F32) + got_v[j].astype(F32) - low).astype(BF16)
        here = pl.ds(s.start, FTILE)
        done += copies(
            out_sems.at[pl.ds(2 * j, 2)],
            [(up_v.at[j], update.at[:, here]), (new_v.at[j], new_err.at[:, here])],
        )
    wait(done)


def final_part(at, inv, rows, own, other, kept, got):
    n = DIM // FTILE
    return call(
        final_kernel,
        "final_part",
        [(at, True), (inv, True), (rows, True), (own, True), (other, True)]
        + [(a, False) for a in (*kept, *got)],
        [((RANK, DIM), F32, True), ((ROWS, DIM), BF16, False), ((ROWS, DIM), BF16, False)],
        [pltpu.VMEM((RANK, DIM), F32)]
        + [pltpu.VMEM((n, ROWS, FTILE), BF16)] * 4
        + [DMA(2 * n), DMA(2 * n)],
        2 * 256 * 256 * 4096,
        8 << 20,
    )


def spread(t, axes):
    n = lax.axis_size(axes)
    return lax.all_to_all(t, axes, 0, 0, tiled=True).reshape(n, -1, 8, 128)


def collect(m, axes):
    n = lax.axis_size(axes)
    return spread(jnp.broadcast_to(m[None], (n,) + m.shape).reshape(-1, 8, 128), axes)


def body(context, cotangent, out_weight, error_buffer, seed_basis):
    x, yl, c = lax.axis_index("x"), lax.axis_index("yl"), lax.axis_index("c")
    at = jnp.stack([x, yl, c]).astype(jnp.int32)
    error = error_buffer[0]

    keep, send = left_part(at, seed_basis.T, cotangent, error, context)
    keep, send, cot, ctx, weight = fence((keep, send, cotangent, context, out_weight))

    wide_a, wide_b = [
        [lax.all_gather(cot[:, a : a + n], "x", axis=0)] for a, n in zip(STARTS, SPLIT)
    ]

    moved = quarters(at, ctx)
    perms = (RIGHT, LEFT, OPPOSITE)
    ctx_x = [moved[0]] + [lax.ppermute(m, "x", p) for m, p in zip(moved[1:], perms)]
    got = spread(keep + lax.ppermute(send, "c", SWAP), "z")
    half = pick_half(at, weight)
    got, ctx_x, half = fence((got, ctx_x, half))

    got = collect(jnp.sum(got, 0), ("yh", "x", "yl"))
    got, half = fence((got, half))

    pt = collect(jnp.sum(got, 0), "z").reshape(-1, 8, 128)
    pt, half = fence((pt, half))
    half = lax.ppermute(half, "yl", SWAP)
    po = lax.ppermute(pt, "c", SWAP)

    keep, send, gram, p_rows = right_part(at, pt, po, context, cotangent, error)
    keep, send, gram = fence((keep, send, gram))
    got = spread(keep + lax.ppermute(send, "c", SWAP), "z")
    kept_a, sent_a = grad_chunk(at, ctx_x, cotangent, error, wide_a, STARTS[0])
    got, kept_a, sent_a, half = fence((got, kept_a, sent_a, half))

    got_a = lax.ppermute(sent_a, "yl", SWAP)
    other = lax.ppermute(half, "c", SWAP)
    got = collect(jnp.sum(got, 0), ("yh", "x", "yl"))
    chol = jnp.linalg.cholesky(gram)
    inv = lax.linalg.triangular_solve(
        chol, jnp.eye(RANK, dtype=F32), left_side=True, lower=True
    )
    got, got_a, inv, other = fence((got, got_a, inv, other))

    qt = collect(jnp.sum(got, 0), "z").reshape(-1, 8, 128)
    kept_b, sent_b = grad_chunk(at, ctx_x, cotangent, error, wide_b, STARTS[1])
    qt, kept_b, sent_b = fence((qt, kept_b, sent_b))

    got_b = lax.ppermute(sent_b, "yl", SWAP)
    qo = lax.ppermute(qt, "c", SWAP)
    groups = list(zip(STARTS, (wide_a, wide_b)))
    blocks = ctx_blocks(at, cotangent, groups, [weight, half, other])
    got_b, qo, blocks = fence((got_b, qo, blocks))
    back = (LEFT, RIGHT, OPPOSITE)
    home = [blocks[0]] + [lax.ppermute(m, "x", p) for m, p in zip(blocks[1:], back)]
    new_basis, update, new_error = final_part(
        at, inv, p_rows, qt, qo, (kept_a, kept_b), (got_a, got_b)
    )
    ctx_grad = place(at, [home[0], home[2], home[1], home[3]])
    return (ctx_grad, update, new_error[None], new_basis.T)


def solution(mesh):
    fine = Mesh(mesh.devices.reshape(2, 8, 2, 4, 2), AXES)
    return jax.shard_map(
        body,
        mesh=fine,
        in_specs=(P(AXES, None), P(AXES, None), P(FSDP, None), P(REP, FSDP, None), P()),
        out_specs=(P(AXES, None), P(FSDP, None), P(REP, FSDP, None), P()),
        check_vma=False,
    )
```

```python
import functools

import jax
import jax.numpy as jnp
from jax import lax
from jax.experimental import pallas as pl
from jax.experimental.pallas import tpu as pltpu
from jax.sharding import Mesh
from jax.sharding import PartitionSpec as P

AXES = ("yh", "z", "c", "x", "yl")
FSDP = ("x", "yl")
REP = ("yh", "z", "c")
F32 = jnp.float32
BF16 = jnp.bfloat16
SWAP = [(0, 1), (1, 0)]
TOK = 256
ROWS = 256
HD = 2048
DIM = 4096
RANK = 32
N_REP = 32
SPLIT = (1536, 1536, 1024)
STARTS = (0, 1536, 3072)
TILE = 512
FTILE = 512
VMEM = 60 << 20
NT = (((1,), (1,)), ((), ()))
NN = (((1,), (0,)), ((), ()))
TN = (((0,), (0,)), ((), ()))
RIGHT = [(0, 1), (1, 2), (2, 3), (3, 0)]
LEFT = [(1, 0), (2, 1), (3, 2), (0, 3)]
OPPOSITE = [(0, 2), (1, 3), (2, 0), (3, 1)]
fence = lax.optimization_barrier


def dot(a, b, dims):
    return lax.dot_general(a, b, dims, preferred_element_type=F32)


def terms(a):
    hi = a.astype(BF16)
    rest = a - hi.astype(F32)
    mid = rest.astype(BF16)
    return hi, mid, (rest - mid.astype(F32)).astype(BF16)


def split3(a):
    return jnp.concatenate(terms(a), axis=0)


def fold3(a):
    n = a.shape[0] // 3
    return a[:n] + (a[n : 2 * n] + a[2 * n :])


def left6(a):
    hi, mid, low = terms(a)
    return jnp.concatenate([hi, hi, mid, hi, mid, low], axis=0)


def right6(a):
    hi, mid, low = terms(a)
    return jnp.concatenate([hi, mid, hi, low, mid, hi], axis=0)


def params(size=VMEM):
    return pltpu.CompilerParams(vmem_limit_bytes=size)


def cost(flops, size):
    return pl.CostEstimate(flops=flops, bytes_accessed=size, transcendentals=0)


def to_tiles(src, row, out):
    lanes = src.shape[1] // 128
    for i in range(2):
        part = src[pl.ds(pl.multiple_of(row + 8 * i, 8), 8), :]
        for j in range(lanes):
            out[i * lanes + j] = part[:, j * 128 : (j + 1) * 128]


def from_tiles(t, row, dst):
    lanes = dst.shape[1] // 128
    for i in range(2):
        for j in range(lanes):
            dst[pl.ds(pl.multiple_of(row + 8 * i, 8), 8), j * 128 : (j + 1) * 128] = t[
                i * lanes + j
            ]


def copies(sems, pairs):
    started = []
    for i, (src, dst) in enumerate(pairs):
        copy = pltpu.make_async_copy(src, dst, sems.at[i])
        copy.start()
        started.append(copy)
    return started


def wait(started):
    for copy in started:
        copy.wait()


def call(kernel, name, ins, outs, scratch, flops, size, alias=None, hide=False):
    spec = lambda inside: pl.BlockSpec(memory_space=pltpu.VMEM if inside else pl.ANY)
    return pl.pallas_call(
        kernel,
        in_specs=[pl.BlockSpec(memory_space=pltpu.SMEM)] + [spec(i) for _, i in ins[1:]],
        out_specs=[spec(i) for _, _, i in outs],
        out_shape=[jax.ShapeDtypeStruct(shape, dtype) for shape, dtype, _ in outs],
        scratch_shapes=scratch,
        input_output_aliases=alias or {},
        compiler_params=params(),
        cost_estimate=cost(flops, size) if hide else cost(1, 1),
        name=name,
    )(*[a for a, _ in ins])


DMA = lambda n: pltpu.SemaphoreType.DMA((n,))
PART = 1024
PARTS = DIM // PART


def left_kernel(at, seed, cot, err, ctx, keep, send, seed_v, cot_v, err_v, ctx_v, p, sems):
    sides = [slice(j * PART, (j + 1) * PART) for j in range(PARTS)]
    started = copies(
        sems,
        [(a.at[:, s], b.at[:, s]) for s in sides for a, b in ((seed, seed_v), (cot, cot_v), (err, err_v))]
        + [(ctx, ctx_v)],
    )
    u = e = 0.0
    for j, s in enumerate(sides):
        wait(started[3 * j : 3 * j + 3])
        s3 = split3(seed_v[:, s])
        u += dot(s3, cot_v[:, s], NT)
        e += dot(s3, err_v[:, s], NT)
    wait(started[-1:])
    p[...] = fold3(dot(split3(fold3(u)), ctx_v[...], NN))
    cols = pl.ds(pl.multiple_of((at[0] * 2 + at[1]) * ROWS, ROWS), ROWS)
    p[:, cols] += fold3(e)
    to_tiles(p, at[2] * 16, keep)
    to_tiles(p, (1 - at[2]) * 16, send)


def left_part(at, seed_t, cot, err, ctx):
    out = ((HD // 64, 8, 128), F32, True)
    return call(
        left_kernel,
        "left_part",
        [(at, True), (seed_t, False), (cot, False), (err, False), (ctx, False)],
        [out, out],
        [
            pltpu.VMEM((RANK, DIM), F32),
            pltpu.VMEM((TOK, DIM), BF16),
            pltpu.VMEM((ROWS, DIM), BF16),
            pltpu.VMEM((TOK, HD), BF16),
            pltpu.VMEM((RANK, HD), F32),
            DMA(3 * PARTS + 1),
        ],
        2 * 256 * 256 * 4096 * 3,
        6 << 20,
    )


def right_kernel(
    at, own, other, ctx, cot, err, keep, send, gram, rows, ctx_v, cot_v, err_v, p, q, sems
):
    sides = [slice(j * PART, (j + 1) * PART) for j in range(PARTS)]
    started = copies(
        sems,
        [(ctx, ctx_v)]
        + [(a.at[:, s], b.at[:, s]) for s in sides for a, b in ((cot, cot_v), (err, err_v))],
    )
    from_tiles(own, at[2] * 16, p)
    from_tiles(other, (1 - at[2]) * 16, p)
    p[...] = p[...] * (1.0 / N_REP)
    p3 = split3(p[...])
    mine = p[:, pl.ds(pl.multiple_of((at[0] * 2 + at[1]) * ROWS, ROWS), ROWS)]
    rows[...] = mine
    r3 = split3(mine)
    full = dot(p3, p3, NT)
    full = full[:RANK] + (full[RANK : 2 * RANK] + full[2 * RANK :])
    gram[...] = full[:, :RANK] + (full[:, RANK : 2 * RANK] + full[:, 2 * RANK :])
    wait(started[:1])
    v3 = split3(fold3(dot(p3, ctx_v[...], NT)))
    for j, s in enumerate(sides):
        wait(started[1 + 2 * j : 3 + 2 * j])
        q[:, s] = fold3(dot(v3, cot_v[:, s], NN) + dot(r3, err_v[:, s], NN))
    to_tiles(q, at[2] * 16, keep)
    to_tiles(q, (1 - at[2]) * 16, send)


def right_part(at, own, other, ctx, cot, err):
    out = ((DIM // 64, 8, 128), F32, True)
    return call(
        right_kernel,
        "right_part",
        [(at, True), (own, True), (other, True), (ctx, False), (cot, False), (err, False)],
        [out, out, ((RANK, RANK), F32, True), ((RANK, ROWS), F32, True)],
        [
            pltpu.VMEM((TOK, HD), BF16),
            pltpu.VMEM((TOK, DIM), BF16),
            pltpu.VMEM((ROWS, DIM), BF16),
            pltpu.VMEM((RANK, HD), F32),
            pltpu.VMEM((RANK, DIM), F32),
            DMA(2 * PARTS + 1),
        ],
        2 * 256 * 256 * 4096 * 3,
        6 << 20,
    )


def quarters_kernel(at, ctx, *rest):
    outs, ctx_v, sems = rest[:4], rest[4], rest[5]
    wait(copies(sems, [(ctx, ctx_v)]))
    for out, k in zip(outs, (0, 1, 3, 2)):
        lane = pl.multiple_of(lax.rem(at[0] + k, 4) * 2 * ROWS, 2 * ROWS)
        out[...] = ctx_v[:, pl.ds(lane, 2 * ROWS)].T


def quarters(at, ctx):
    return call(
        quarters_kernel,
        "quarters",
        [(at, True), (ctx, False)],
        [((2 * ROWS, TOK), BF16, True)] * 4,
        [pltpu.VMEM((TOK, HD), BF16), DMA(1)],
        0,
        2 << 20,
    )


def pick_kernel(at, src, dst, sems):
    n, cols = dst.shape
    rows = pl.ds(pl.multiple_of(at[2] * n, n), n)
    width = cols // 4
    sides = [pl.ds(i * width, width) for i in range(4)]
    wait(copies(sems, [(src.at[rows, s], dst.at[:, s]) for s in sides]))


def pick_half(at, a):
    rows, cols = a.shape
    outs = [((rows // 2, cols), a.dtype, True)]
    return call(pick_kernel, "pick_half", [(at, True), (a, False)], outs, [DMA(4)], 0, 2 << 20)[0]


def block_pairs(at, col, cot, wide, buf):
    cols = pl.ds(col, TILE)
    pairs = [(cot.at[:, cols], buf.at[pl.ds(0, TOK)])]
    for i, k in enumerate((3, 1, 2)):
        src = wide.at[lax.rem(at[0] + k, 4), :, cols]
        pairs.append((src, buf.at[pl.ds((i + 1) * TOK, TOK)]))
    return pairs


def grad_kernel(start, count, at, *refs):
    ctx, cot, err, wide, kept, sent = refs[:4], *refs[4:9]
    lhs, buf, err_v, out_k, out_s, in_sems, out_sems = refs[9:]
    yl = at[1]
    pairs = []
    for k, block in enumerate(ctx):
        for i, row in enumerate((yl, 1 - yl)):
            rows = pl.ds(pl.multiple_of(row * ROWS, ROWS), ROWS)
            to = lhs.at[pl.ds(i * ROWS, ROWS), pl.ds(k * TOK, TOK)]
            pairs.append((block.at[rows, :], to))
    for j in range(count):
        col = start + j * TILE
        pairs += block_pairs(at, col, cot, wide, buf.at[j])
        pairs.append((err.at[:, pl.ds(col, TILE)], err_v.at[j]))
    started = copies(in_sems, pairs)
    wait(started[:8])
    done = []
    for j in range(count):
        wait(started[8 + 5 * j : 13 + 5 * j])
        out = dot(lhs[...], buf[j], NN)
        out_k[j] = (out[:ROWS] + err_v[j].astype(F32)).astype(BF16)
        out_s[j] = out[ROWS:].astype(BF16)
        here = pl.ds(j * TILE, TILE)
        done += copies(
            out_sems.at[pl.ds(2 * j, 2)],
            [(out_k.at[j], kept.at[:, here]), (out_s.at[j], sent.at[:, here])],
        )
    wait(done)


def grad_chunk(at, ctx, cot, err, wide, start, width):
    count = width // TILE
    return call(
        functools.partial(grad_kernel, start, count),
        "grad_chunk",
        [(at, True)] + [(a, False) for a in (*ctx, cot, err, wide)],
        [((ROWS, width), BF16, False)] * 2,
        [
            pltpu.VMEM((2 * ROWS, 4 * TOK), BF16),
            pltpu.VMEM((count, 4 * TOK, TILE), BF16),
            pltpu.VMEM((count, ROWS, TILE), BF16),
            pltpu.VMEM((count, ROWS, TILE), BF16),
            pltpu.VMEM((count, ROWS, TILE), BF16),
            DMA(8 + 5 * count),
            DMA(2 * count),
        ],
        2 * 512 * 1024 * width,
        4 * 1024 * width,
        hide=True,
    )


def ctx_kernel(at, cot, w_own, w_half, w_other, wide, *refs):
    outs, (buf, wbuf, acc, sems) = refs[:4], refs[4:]
    half = ROWS // 2
    count = DIM // TILE
    pairs = []
    for j in range(count):
        pairs += block_pairs(at, j * TILE, cot, wide, buf.at[j])
        cols = pl.ds(j * TILE, TILE)
        for w, row, m in ((w_own, 0, ROWS), (w_half, ROWS, half), (w_other, ROWS + half, half)):
            pairs.append((w.at[:, cols], wbuf.at[j, pl.ds(row, m)]))
    started = copies(sems, pairs)
    for j in range(count):
        wait(started[7 * j : 7 * j + 7])
        part = dot(buf[j], wbuf[j], NT)
        if j == 0:
            acc[...] = part
        else:
            acc[...] += part
    yl, c = at[1], at[2]
    mine = pl.ds(pl.multiple_of(yl * ROWS, ROWS), ROWS)
    for k, out in enumerate(outs):
        tok = slice(k * TOK, (k + 1) * TOK)
        out[:, mine] = acc[tok, :ROWS].astype(BF16)
        for i, h in enumerate((c, 1 - c)):
            lane = pl.multiple_of((1 - yl) * ROWS + h * half, half)
            out[:, pl.ds(lane, half)] = acc[tok, ROWS + i * half : ROWS + (i + 1) * half].astype(
                BF16
            )


def ctx_blocks(at, cot, wide, weights):
    count = DIM // TILE
    return call(
        ctx_kernel,
        "ctx_blocks",
        [(at, True)] + [(a, False) for a in (cot, *weights, wide)],
        [((TOK, 2 * ROWS), BF16, True)] * 4,
        [
            pltpu.VMEM((count, 4 * TOK, TILE), BF16),
            pltpu.VMEM((count, 2 * ROWS, TILE), BF16),
            pltpu.VMEM((4 * TOK, 2 * ROWS), F32),
            DMA(7 * count),
        ],
        2 * 512 * 1024 * DIM,
        4 * 1024 * DIM,
    )


def final_kernel(at, inv, rows, own, other, *refs):
    kept, got, refs = refs[:2], refs[2:4], refs[4:]
    basis, pb, update, new_err, q, nb6, kept_v, got_v, up_v, new_v = refs[:10]
    in_sems, up_sems, new_sems = refs[10:]
    sides = [pl.ds(j * FTILE, FTILE) for j in range(DIM // FTILE)]
    known = STARTS[2] // FTILE
    pairs = []
    for j in range(known):
        i = 1 if j * FTILE >= STARTS[1] else 0
        src = pl.ds(j * FTILE - STARTS[i], FTILE)
        pairs += [(kept[i].at[:, src], kept_v.at[j]), (got[i].at[:, src], got_v.at[j])]
    started = copies(in_sems, pairs)
    from_tiles(own, at[2] * 16, q)
    from_tiles(other, (1 - at[2]) * 16, q)
    inv6 = left6(inv[...].T)
    pb[...] = left6(dot(inv6, right6(rows[...]), TN))
    nb = dot(inv6, right6(q[...]), TN) * (1.0 / N_REP)
    basis[...] = nb
    nb6[...] = right6(nb)
    done = []
    for j, s in enumerate(sides):
        low = dot(pb[...], nb6[:, s], TN)
        up_v[j] = low.astype(BF16)
        done += copies(up_sems.at[pl.ds(j, 1)], [(up_v.at[j], update.at[:, s])])
        if j < known:
            wait(started[2 * j : 2 * j + 2])
            new_v[j] = (kept_v[j].astype(F32) + got_v[j].astype(F32) - low).astype(BF16)
            done += copies(new_sems.at[pl.ds(j, 1)], [(new_v.at[j], new_err.at[:, s])])
    wait(done)


def final_part(at, inv, rows, own, other, kept, got):
    n, known = DIM // FTILE, STARTS[2] // FTILE
    wide = lambda k: pltpu.VMEM((k, ROWS, FTILE), BF16)
    return call(
        final_kernel,
        "final_part",
        [(at, True), (inv, True), (rows, True), (own, True), (other, True)]
        + [(a, False) for a in (*kept, *got)],
        [
            ((RANK, DIM), F32, True),
            ((6 * RANK, ROWS), BF16, True),
            ((ROWS, DIM), BF16, False),
            ((ROWS, DIM), BF16, False),
        ],
        [pltpu.VMEM((RANK, DIM), F32), pltpu.VMEM((6 * RANK, DIM), BF16)]
        + [wide(known), wide(known), wide(n), wide(known)]
        + [DMA(2 * known), DMA(n), DMA(known)],
        2 * 256 * 256 * 4096,
        8 << 20,
    )


def last_kernel(at, basis, pb, kept, got, *refs):
    parts, new_err, grad = refs[:4], refs[5], refs[6]
    kept_v, got_v, new_v, part_v, sems, new_sems, part_sems, grad_sems = refs[7:]
    count = SPLIT[2] // FTILE
    pairs = []
    for j in range(count):
        src = pl.ds(j * FTILE, FTILE)
        pairs += [(kept.at[:, src], kept_v.at[j]), (got.at[:, src], got_v.at[j])]
    started = copies(sems, pairs)
    arriving = copies(part_sems, [(part, part_v.at[i]) for i, part in enumerate(parts)])
    done = []
    for j in range(count):
        s = pl.ds(STARTS[2] + j * FTILE, FTILE)
        low = dot(pb[...], right6(basis[:, s]), TN)
        wait(started[2 * j : 2 * j + 2])
        new_v[j] = (kept_v[j].astype(F32) + got_v[j].astype(F32) - low).astype(BF16)
        done += copies(new_sems.at[pl.ds(j, 1)], [(new_v.at[j], new_err.at[:, s])])
    width = 2 * ROWS
    for i, k in enumerate((0, 3, 1, 2)):
        lane = pl.multiple_of(lax.rem(at[0] + k, 4) * width, width)
        wait(arriving[i : i + 1])
        done += copies(
            grad_sems.at[pl.ds(i, 1)], [(part_v.at[i], grad.at[:, pl.ds(lane, width)])]
        )
    wait(done)


def last_part(at, basis, pb, kept, got, parts, partial):
    count = SPLIT[2] // FTILE
    return call(
        last_kernel,
        "last_part",
        [(at, True), (basis, True), (pb, True)]
        + [(a, False) for a in (kept, got, *parts, partial)],
        [((ROWS, DIM), BF16, False), ((TOK, HD), BF16, False)],
        [pltpu.VMEM((count, ROWS, FTILE), BF16)] * 3
        + [pltpu.VMEM((4, TOK, 2 * ROWS), BF16)]
        + [DMA(2 * count), DMA(count), DMA(4), DMA(4)],
        2 * 256 * 256 * 1024,
        4 << 20,
        {9: 0},
    )


def spread(t, axes):
    n = lax.axis_size(axes)
    return lax.all_to_all(t, axes, 0, 0, tiled=True).reshape(n, -1, 8, 128)


def copies_for(m, axes):
    n = lax.axis_size(axes)
    return jnp.broadcast_to(m[None], (n,) + m.shape).reshape(-1, 8, 128)


def collect(m, axes):
    return spread(copies_for(m, axes), axes)


def body(context, cotangent, out_weight, error_buffer, seed_basis):
    x, yl, c = lax.axis_index("x"), lax.axis_index("yl"), lax.axis_index("c")
    at = jnp.stack([x, yl, c]).astype(jnp.int32)
    error = error_buffer[0]

    wide = lax.all_gather(cotangent, "x", axis=0)

    keep, send = left_part(at, seed_basis.T, cotangent, error, context)
    keep, send, ctx, weight = fence((keep, send, context, out_weight))

    moved = quarters(at, ctx)
    perms = (RIGHT, LEFT, OPPOSITE)
    ctx_x = [moved[0]] + [lax.ppermute(m, "x", p) for m, p in zip(moved[1:], perms)]
    got = spread(keep + lax.ppermute(send, "c", SWAP), "z")
    half = pick_half(at, weight)
    got, ctx_x, half = fence((got, ctx_x, half))

    got = collect(jnp.sum(got, 0), ("yh", "x", "yl"))
    got, half = fence((got, half))

    pt = collect(jnp.sum(got, 0), "z").reshape(-1, 8, 128)
    pt, half = fence((pt, half))
    half = lax.ppermute(half, "yl", SWAP)
    po = lax.ppermute(pt, "c", SWAP)

    keep, send, gram, p_rows = right_part(at, pt, po, context, cotangent, error)
    keep, send, gram = fence((keep, send, gram))
    got = spread(keep + lax.ppermute(send, "c", SWAP), "z")
    chol = jnp.linalg.cholesky(gram)
    inv = lax.linalg.triangular_solve(
        chol, jnp.eye(RANK, dtype=F32), left_side=True, lower=True
    )
    got, inv, half = fence((got, inv, half))

    other = lax.ppermute(half, "c", SWAP)
    got = collect(jnp.sum(got, 0), ("yh", "x", "yl"))
    grad = lambda i: grad_chunk(at, ctx_x, cotangent, error, wide, STARTS[i], SPLIT[i])
    kept_a, sent_a = grad(0)
    got, other, kept_a, sent_a = fence((got, other, kept_a, sent_a))

    got_a = lax.ppermute(sent_a, "yl", SWAP)
    out, late = fence((copies_for(jnp.sum(got, 0), "z"), wide))
    qt = spread(out, "z").reshape(-1, 8, 128)
    grad = lambda i: grad_chunk(at, ctx_x, cotangent, error, late, STARTS[i], SPLIT[i])
    kept_b, sent_b = grad(1)
    got_b = lax.ppermute(sent_b, "yl", SWAP)
    kept_c, sent_c = grad(2)
    qt, kept_b, kept_c, sent_c = fence((qt, kept_b, kept_c, sent_c))

    got_c = lax.ppermute(sent_c, "yl", SWAP)
    qo = lax.ppermute(qt, "c", SWAP)
    blocks = ctx_blocks(at, cotangent, wide, [weight, half, other])
    qo, blocks = fence((qo, blocks))
    back = (LEFT, RIGHT, OPPOSITE)
    home = [blocks[0]] + [lax.ppermute(m, "x", p) for m, p in zip(blocks[1:], back)]
    new_basis, pb, update, partial = final_part(
        at, inv, p_rows, qt, qo, (kept_a, kept_b), (got_a, got_b)
    )
    new_basis, got_c, home, partial = fence((new_basis, got_c, home, partial))
    parts = [home[0], home[2], home[1], home[3]]
    new_error, ctx_grad = last_part(at, new_basis, pb, kept_c, got_c, parts, partial)
    return (ctx_grad, update, new_error[None], new_basis.T)


def solution(mesh):
    fine = Mesh(mesh.devices.reshape(2, 8, 2, 4, 2), AXES)
    return jax.shard_map(
        body,
        mesh=fine,
        in_specs=(P(AXES, None), P(AXES, None), P(FSDP, None), P(REP, FSDP, None), P()),
        out_specs=(P(AXES, None), P(FSDP, None), P(REP, FSDP, None), P()),
        check_vma=False,
    )
```

```python
import functools

import jax
import jax.numpy as jnp
from jax import lax
from jax.experimental import pallas as pl
from jax.experimental.pallas import tpu as pltpu
from jax.sharding import Mesh
from jax.sharding import PartitionSpec as P

AXES = ("yh", "z", "c", "x", "yl")
FSDP = ("x", "yl")
REP = ("yh", "z", "c")
F32 = jnp.float32
BF16 = jnp.bfloat16
SWAP = [(0, 1), (1, 0)]
TOK = 256
ROWS = 256
HD = 2048
DIM = 4096
RANK = 32
N_REP = 32
SPLIT = (1536, 1536, 1024)
STARTS = (0, 1536, 3072)
TILE = 512
FTILE = 512
VMEM = 60 << 20
NT = (((1,), (1,)), ((), ()))
NN = (((1,), (0,)), ((), ()))
TN = (((0,), (0,)), ((), ()))
RIGHT = [(0, 1), (1, 2), (2, 3), (3, 0)]
LEFT = [(1, 0), (2, 1), (3, 2), (0, 3)]
OPPOSITE = [(0, 2), (1, 3), (2, 0), (3, 1)]
fence = lax.optimization_barrier


def dot(a, b, dims):
    return lax.dot_general(a, b, dims, preferred_element_type=F32)


def terms(a):
    hi = a.astype(BF16)
    rest = a - hi.astype(F32)
    mid = rest.astype(BF16)
    return hi, mid, (rest - mid.astype(F32)).astype(BF16)


def split3(a):
    return jnp.concatenate(terms(a), axis=0)


def fold3(a):
    n = a.shape[0] // 3
    return a[:n] + (a[n : 2 * n] + a[2 * n :])


def left6(a):
    hi, mid, low = terms(a)
    return jnp.concatenate([hi, hi, mid, hi, mid, low], axis=0)


def right6(a):
    hi, mid, low = terms(a)
    return jnp.concatenate([hi, mid, hi, low, mid, hi], axis=0)


def params(size=VMEM):
    return pltpu.CompilerParams(vmem_limit_bytes=size)


def cost(flops, size):
    return pl.CostEstimate(flops=flops, bytes_accessed=size, transcendentals=0)


def to_tiles(src, row, out):
    lanes = src.shape[1] // 128
    for i in range(2):
        part = src[pl.ds(pl.multiple_of(row + 8 * i, 8), 8), :]
        for j in range(lanes):
            out[i * lanes + j] = part[:, j * 128 : (j + 1) * 128]


def from_tiles(t, row, dst):
    lanes = dst.shape[1] // 128
    for i in range(2):
        for j in range(lanes):
            dst[pl.ds(pl.multiple_of(row + 8 * i, 8), 8), j * 128 : (j + 1) * 128] = t[
                i * lanes + j
            ]


def copies(sems, pairs):
    started = []
    for i, (src, dst) in enumerate(pairs):
        copy = pltpu.make_async_copy(src, dst, sems.at[i])
        copy.start()
        started.append(copy)
    return started


def wait(started):
    for copy in started:
        copy.wait()


def call(kernel, name, ins, outs, scratch, flops, size, alias=None, hide=False, vmem=VMEM):
    spec = lambda inside: pl.BlockSpec(memory_space=pltpu.VMEM if inside else pl.ANY)
    return pl.pallas_call(
        kernel,
        in_specs=[pl.BlockSpec(memory_space=pltpu.SMEM)] + [spec(i) for _, i in ins[1:]],
        out_specs=[spec(i) for _, _, i in outs],
        out_shape=[jax.ShapeDtypeStruct(shape, dtype) for shape, dtype, _ in outs],
        scratch_shapes=scratch,
        input_output_aliases=alias or {},
        compiler_params=params(vmem),
        cost_estimate=cost(flops, size) if hide else cost(1, 1),
        name=name,
    )(*[a for a, _ in ins])


DMA = lambda n: pltpu.SemaphoreType.DMA((n,))
PART = 1024
PARTS = DIM // PART


def left_kernel(at, seed, cot, err, ctx, keep, send, seed_v, cot_v, err_v, ctx_v, p, sems):
    sides = [slice(j * PART, (j + 1) * PART) for j in range(PARTS)]
    started = copies(
        sems,
        [(a.at[:, s], b.at[:, s]) for s in sides for a, b in ((seed, seed_v), (cot, cot_v), (err, err_v))]
        + [(ctx, ctx_v)],
    )
    u = e = 0.0
    for j, s in enumerate(sides):
        wait(started[3 * j : 3 * j + 3])
        s3 = split3(seed_v[:, s])
        u += dot(s3, cot_v[:, s], NT)
        e += dot(s3, err_v[:, s], NT)
    wait(started[-1:])
    p[...] = fold3(dot(split3(fold3(u)), ctx_v[...], NN))
    cols = pl.ds(pl.multiple_of((at[0] * 2 + at[1]) * ROWS, ROWS), ROWS)
    p[:, cols] += fold3(e)
    to_tiles(p, at[2] * 16, keep)
    to_tiles(p, (1 - at[2]) * 16, send)


def left_part(at, seed_t, cot, err, ctx):
    out = ((HD // 64, 8, 128), F32, True)
    return call(
        left_kernel,
        "left_part",
        [(at, True), (seed_t, False), (cot, False), (err, False), (ctx, False)],
        [out, out],
        [
            pltpu.VMEM((RANK, DIM), F32),
            pltpu.VMEM((TOK, DIM), BF16),
            pltpu.VMEM((ROWS, DIM), BF16),
            pltpu.VMEM((TOK, HD), BF16),
            pltpu.VMEM((RANK, HD), F32),
            DMA(3 * PARTS + 1),
        ],
        2 * 256 * 256 * 4096 * 3,
        6 << 20,
    )


def right_kernel(
    at, own, other, ctx, cot, err, keep, send, gram, rows, ctx_v, cot_v, err_v, p, q, sems
):
    sides = [slice(j * PART, (j + 1) * PART) for j in range(PARTS)]
    started = copies(
        sems,
        [(ctx, ctx_v)]
        + [(a.at[:, s], b.at[:, s]) for s in sides for a, b in ((cot, cot_v), (err, err_v))],
    )
    from_tiles(own, at[2] * 16, p)
    from_tiles(other, (1 - at[2]) * 16, p)
    p[...] = p[...] * (1.0 / N_REP)
    p3 = split3(p[...])
    mine = p[:, pl.ds(pl.multiple_of((at[0] * 2 + at[1]) * ROWS, ROWS), ROWS)]
    rows[...] = mine
    r3 = split3(mine)
    full = dot(p3, p3, NT)
    full = full[:RANK] + (full[RANK : 2 * RANK] + full[2 * RANK :])
    gram[...] = full[:, :RANK] + (full[:, RANK : 2 * RANK] + full[:, 2 * RANK :])
    wait(started[:1])
    v3 = split3(fold3(dot(p3, ctx_v[...], NT)))
    for j, s in enumerate(sides):
        wait(started[1 + 2 * j : 3 + 2 * j])
        q[:, s] = fold3(dot(v3, cot_v[:, s], NN) + dot(r3, err_v[:, s], NN))
    to_tiles(q, at[2] * 16, keep)
    to_tiles(q, (1 - at[2]) * 16, send)


def right_part(at, own, other, ctx, cot, err):
    out = ((DIM // 64, 8, 128), F32, True)
    return call(
        right_kernel,
        "right_part",
        [(at, True), (own, True), (other, True), (ctx, False), (cot, False), (err, False)],
        [out, out, ((RANK, RANK), F32, True), ((RANK, ROWS), F32, True)],
        [
            pltpu.VMEM((TOK, HD), BF16),
            pltpu.VMEM((TOK, DIM), BF16),
            pltpu.VMEM((ROWS, DIM), BF16),
            pltpu.VMEM((RANK, HD), F32),
            pltpu.VMEM((RANK, DIM), F32),
            DMA(2 * PARTS + 1),
        ],
        2 * 256 * 256 * 4096 * 3,
        6 << 20,
    )


def quarters_kernel(at, ctx, *rest):
    outs, ctx_v, sems = rest[:4], rest[4], rest[5]
    wait(copies(sems, [(ctx, ctx_v)]))
    for out, k in zip(outs, (0, 1, 3, 2)):
        lane = pl.multiple_of(lax.rem(at[0] + k, 4) * 2 * ROWS, 2 * ROWS)
        out[...] = ctx_v[:, pl.ds(lane, 2 * ROWS)].T


def quarters(at, ctx):
    return call(
        quarters_kernel,
        "quarters",
        [(at, True), (ctx, False)],
        [((2 * ROWS, TOK), BF16, True)] * 4,
        [pltpu.VMEM((TOK, HD), BF16), DMA(1)],
        0,
        2 << 20,
    )


def pick_kernel(at, src, dst, sems):
    n, cols = dst.shape
    rows = pl.ds(pl.multiple_of(at[2] * n, n), n)
    width = cols // 4
    sides = [pl.ds(i * width, width) for i in range(4)]
    wait(copies(sems, [(src.at[rows, s], dst.at[:, s]) for s in sides]))


def pick_half(at, a):
    rows, cols = a.shape
    outs = [((rows // 2, cols), a.dtype, True)]
    return call(pick_kernel, "pick_half", [(at, True), (a, False)], outs, [DMA(4)], 0, 2 << 20)[0]


def block_pairs(at, col, cot, wide, buf):
    cols = pl.ds(col, TILE)
    pairs = [(cot.at[:, cols], buf.at[pl.ds(0, TOK)])]
    for i, k in enumerate((3, 1, 2)):
        src = wide.at[lax.rem(at[0] + k, 4), :, cols]
        pairs.append((src, buf.at[pl.ds((i + 1) * TOK, TOK)]))
    return pairs


def grad_kernel(start, count, at, *refs):
    ctx, cot, err, wide, kept, sent = refs[:4], *refs[4:9]
    lhs, buf, err_v, out_k, out_s, in_sems, out_sems = refs[9:]
    yl = at[1]
    pairs = []
    for k, block in enumerate(ctx):
        for i, row in enumerate((yl, 1 - yl)):
            rows = pl.ds(pl.multiple_of(row * ROWS, ROWS), ROWS)
            to = lhs.at[pl.ds(i * ROWS, ROWS), pl.ds(k * TOK, TOK)]
            pairs.append((block.at[rows, :], to))
    for j in range(count):
        col = start + j * TILE
        pairs += block_pairs(at, col, cot, wide, buf.at[j])
        pairs.append((err.at[:, pl.ds(col, TILE)], err_v.at[j]))
    started = copies(in_sems, pairs)
    wait(started[:8])
    done = []
    for j in range(count):
        wait(started[8 + 5 * j : 13 + 5 * j])
        out = dot(lhs[...], buf[j], NN)
        out_k[j] = (out[:ROWS] + err_v[j].astype(F32)).astype(BF16)
        out_s[j] = out[ROWS:].astype(BF16)
        here = pl.ds(j * TILE, TILE)
        done += copies(
            out_sems.at[pl.ds(2 * j, 2)],
            [(out_k.at[j], kept.at[:, here]), (out_s.at[j], sent.at[:, here])],
        )
    wait(done)


def grad_chunk(at, ctx, cot, err, wide, start, width):
    count = width // TILE
    return call(
        functools.partial(grad_kernel, start, count),
        "grad_chunk",
        [(at, True)] + [(a, False) for a in (*ctx, cot, err, wide)],
        [((ROWS, width), BF16, False)] * 2,
        [
            pltpu.VMEM((2 * ROWS, 4 * TOK), BF16),
            pltpu.VMEM((count, 4 * TOK, TILE), BF16),
            pltpu.VMEM((count, ROWS, TILE), BF16),
            pltpu.VMEM((count, ROWS, TILE), BF16),
            pltpu.VMEM((count, ROWS, TILE), BF16),
            DMA(8 + 5 * count),
            DMA(2 * count),
        ],
        2 * 512 * 1024 * width,
        4 * 1024 * width,
        hide=True,
    )


def ctx_kernel(at, cot, w_own, w_half, w_other, wide, *refs):
    outs, (buf, wbuf, acc, sems) = refs[:4], refs[4:]
    half = ROWS // 2
    count = DIM // TILE
    pairs = []
    for j in range(count):
        pairs += block_pairs(at, j * TILE, cot, wide, buf.at[j])
        cols = pl.ds(j * TILE, TILE)
        for w, row, m in ((w_own, 0, ROWS), (w_half, ROWS, half), (w_other, ROWS + half, half)):
            pairs.append((w.at[:, cols], wbuf.at[j, pl.ds(row, m)]))
    started = copies(sems, pairs)
    for j in range(count):
        wait(started[7 * j : 7 * j + 7])
        part = dot(buf[j], wbuf[j], NT)
        if j == 0:
            acc[...] = part
        else:
            acc[...] += part
    yl, c = at[1], at[2]
    mine = pl.ds(pl.multiple_of(yl * ROWS, ROWS), ROWS)
    for k, out in enumerate(outs):
        tok = slice(k * TOK, (k + 1) * TOK)
        out[:, mine] = acc[tok, :ROWS].astype(BF16)
        for i, h in enumerate((c, 1 - c)):
            lane = pl.multiple_of((1 - yl) * ROWS + h * half, half)
            out[:, pl.ds(lane, half)] = acc[tok, ROWS + i * half : ROWS + (i + 1) * half].astype(
                BF16
            )


def ctx_blocks(at, cot, wide, weights):
    count = DIM // TILE
    return call(
        ctx_kernel,
        "ctx_blocks",
        [(at, True)] + [(a, False) for a in (cot, *weights, wide)],
        [((TOK, 2 * ROWS), BF16, True)] * 4,
        [
            pltpu.VMEM((count, 4 * TOK, TILE), BF16),
            pltpu.VMEM((count, 2 * ROWS, TILE), BF16),
            pltpu.VMEM((4 * TOK, 2 * ROWS), F32),
            DMA(7 * count),
        ],
        2 * 512 * 1024 * DIM,
        4 * 1024 * DIM,
    )


def final_kernel(at, inv, rows, own, other, *refs):
    kept, got, refs = refs[:2], refs[2:4], refs[4:]
    basis, pb, update, new_err, q, nb6, kept_v, got_v, up_v, new_v = refs[:10]
    in_sems, up_sems, new_sems = refs[10:]
    sides = [pl.ds(j * FTILE, FTILE) for j in range(DIM // FTILE)]
    known = STARTS[2] // FTILE
    pairs = []
    for j in range(known):
        i = 1 if j * FTILE >= STARTS[1] else 0
        src = pl.ds(j * FTILE - STARTS[i], FTILE)
        pairs += [(kept[i].at[:, src], kept_v.at[j]), (got[i].at[:, src], got_v.at[j])]
    started = copies(in_sems, pairs)
    from_tiles(own, at[2] * 16, q)
    from_tiles(other, (1 - at[2]) * 16, q)
    inv6 = left6(inv[...].T)
    pb[...] = left6(dot(inv6, right6(rows[...]), TN))
    nb = dot(inv6, right6(q[...]), TN) * (1.0 / N_REP)
    basis[...] = nb
    nb6[...] = right6(nb)
    done = []
    for j, s in enumerate(sides):
        low = dot(pb[...], nb6[:, s], TN)
        up_v[j] = low.astype(BF16)
        done += copies(up_sems.at[pl.ds(j, 1)], [(up_v.at[j], update.at[:, s])])
        if j < known:
            wait(started[2 * j : 2 * j + 2])
            new_v[j] = (kept_v[j].astype(F32) + got_v[j].astype(F32) - low).astype(BF16)
            done += copies(new_sems.at[pl.ds(j, 1)], [(new_v.at[j], new_err.at[:, s])])
    wait(done)


def final_part(at, inv, rows, own, other, kept, got):
    n, known = DIM // FTILE, STARTS[2] // FTILE
    wide = lambda k: pltpu.VMEM((k, ROWS, FTILE), BF16)
    return call(
        final_kernel,
        "final_part",
        [(at, True), (inv, True), (rows, True), (own, True), (other, True)]
        + [(a, False) for a in (*kept, *got)],
        [
            ((RANK, DIM), F32, True),
            ((6 * RANK, ROWS), BF16, True),
            ((ROWS, DIM), BF16, False),
            ((ROWS, DIM), BF16, False),
        ],
        [pltpu.VMEM((RANK, DIM), F32), pltpu.VMEM((6 * RANK, DIM), BF16)]
        + [wide(known), wide(known), wide(n), wide(known)]
        + [DMA(2 * known), DMA(n), DMA(known)],
        2 * 256 * 256 * 4096,
        8 << 20,
    )


def last_kernel(at, basis, pb, kept, got, *refs):
    parts, new_err, grad = refs[:4], refs[5], refs[6]
    kept_v, got_v, new_v, part_v, sems, new_sems, part_sems, grad_sems = refs[7:]
    count = SPLIT[2] // FTILE
    pairs = []
    for j in range(count):
        src = pl.ds(j * FTILE, FTILE)
        pairs += [(kept.at[:, src], kept_v.at[j]), (got.at[:, src], got_v.at[j])]
    started = copies(sems, pairs)
    arriving = copies(part_sems, [(part, part_v.at[i]) for i, part in enumerate(parts)])
    done = []
    for j in range(count):
        s = pl.ds(STARTS[2] + j * FTILE, FTILE)
        low = dot(pb[...], right6(basis[:, s]), TN)
        wait(started[2 * j : 2 * j + 2])
        new_v[j] = (kept_v[j].astype(F32) + got_v[j].astype(F32) - low).astype(BF16)
        done += copies(new_sems.at[pl.ds(j, 1)], [(new_v.at[j], new_err.at[:, s])])
    width = 2 * ROWS
    for i, k in enumerate((0, 3, 1, 2)):
        lane = pl.multiple_of(lax.rem(at[0] + k, 4) * width, width)
        wait(arriving[i : i + 1])
        done += copies(
            grad_sems.at[pl.ds(i, 1)], [(part_v.at[i], grad.at[:, pl.ds(lane, width)])]
        )
    wait(done)


def last_part(at, basis, pb, kept, got, parts, partial):
    count = SPLIT[2] // FTILE
    return call(
        last_kernel,
        "last_part",
        [(at, True), (basis, True), (pb, True)]
        + [(a, False) for a in (kept, got, *parts, partial)],
        [((ROWS, DIM), BF16, False), ((TOK, HD), BF16, False)],
        [pltpu.VMEM((count, ROWS, FTILE), BF16)] * 3
        + [pltpu.VMEM((4, TOK, 2 * ROWS), BF16)]
        + [DMA(2 * count), DMA(count), DMA(4), DMA(4)],
        2 * 256 * 256 * 1024,
        4 << 20,
        {9: 0},
        vmem=8 << 20,
    )


def spread(t, axes):
    n = lax.axis_size(axes)
    return lax.all_to_all(t, axes, 0, 0, tiled=True).reshape(n, -1, 8, 128)


def copies_for(m, axes):
    n = lax.axis_size(axes)
    return jnp.broadcast_to(m[None], (n,) + m.shape).reshape(-1, 8, 128)


def collect(m, axes):
    return spread(copies_for(m, axes), axes)


def body(context, cotangent, out_weight, error_buffer, seed_basis):
    x, yl, c = lax.axis_index("x"), lax.axis_index("yl"), lax.axis_index("c")
    at = jnp.stack([x, yl, c]).astype(jnp.int32)
    error = error_buffer[0]

    wide = lax.all_gather(cotangent, "x", axis=0)

    keep, send = left_part(at, seed_basis.T, cotangent, error, context)
    keep, send, ctx, weight = fence((keep, send, context, out_weight))

    moved = quarters(at, ctx)
    perms = (RIGHT, LEFT, OPPOSITE)
    ctx_x = [moved[0]] + [lax.ppermute(m, "x", p) for m, p in zip(moved[1:], perms)]
    got = spread(keep + lax.ppermute(send, "c", SWAP), "z")
    half = pick_half(at, weight)
    got, ctx_x, half = fence((got, ctx_x, half))

    got = collect(jnp.sum(got, 0), ("yh", "x", "yl"))
    got, half = fence((got, half))

    pt = collect(jnp.sum(got, 0), "z").reshape(-1, 8, 128)
    pt, half = fence((pt, half))
    half = lax.ppermute(half, "yl", SWAP)
    po = lax.ppermute(pt, "c", SWAP)

    keep, send, gram, p_rows = right_part(at, pt, po, context, cotangent, error)
    keep, send, gram = fence((keep, send, gram))
    got = spread(keep + lax.ppermute(send, "c", SWAP), "z")
    chol = jnp.linalg.cholesky(gram)
    inv = lax.linalg.triangular_solve(
        chol, jnp.eye(RANK, dtype=F32), left_side=True, lower=True
    )
    got, inv, half = fence((got, inv, half))

    other = lax.ppermute(half, "c", SWAP)
    got = collect(jnp.sum(got, 0), ("yh", "x", "yl"))
    grad = lambda i: grad_chunk(at, ctx_x, cotangent, error, wide, STARTS[i], SPLIT[i])
    kept_a, sent_a = grad(0)
    got, other, kept_a = fence((got, other, kept_a))

    got_a = lax.ppermute(sent_a, "yl", SWAP)
    out, late = fence((copies_for(jnp.sum(got, 0), "z"), wide))
    qt = spread(out, "z").reshape(-1, 8, 128)
    grad = lambda i: grad_chunk(at, ctx_x, cotangent, error, late, STARTS[i], SPLIT[i])
    kept_b, sent_b = grad(1)
    got_b = lax.ppermute(sent_b, "yl", SWAP)
    kept_c, sent_c = grad(2)
    qt, kept_b, kept_c, sent_c = fence((qt, kept_b, kept_c, sent_c))

    got_c = lax.ppermute(sent_c, "yl", SWAP)
    qo = lax.ppermute(qt, "c", SWAP)
    blocks = ctx_blocks(at, cotangent, wide, [weight, half, other])
    qo, blocks, got_a = fence((qo, blocks, got_a))
    back = (LEFT, RIGHT, OPPOSITE)
    home = [blocks[0]] + [lax.ppermute(m, "x", p) for m, p in zip(blocks[1:], back)]
    new_basis, pb, update, partial = final_part(
        at, inv, p_rows, qt, qo, (kept_a, kept_b), (got_a, got_b)
    )
    new_basis, got_c, home, partial = fence((new_basis, got_c, home, partial))
    parts = [home[0], home[2], home[1], home[3]]
    new_error, ctx_grad = last_part(at, new_basis, pb, kept_c, got_c, parts, partial)
    return (ctx_grad, update, new_error[None], new_basis.T)


def solution(mesh):
    fine = Mesh(mesh.devices.reshape(2, 8, 2, 4, 2), AXES)
    return jax.shard_map(
        body,
        mesh=fine,
        in_specs=(P(AXES, None), P(AXES, None), P(FSDP, None), P(REP, FSDP, None), P()),
        out_specs=(P(AXES, None), P(FSDP, None), P(REP, FSDP, None), P()),
        check_vma=False,
    )
```
